256 devices in a mesh: dp: 32 (over y, x, core), fsdp: 8 (over z).
Axes of the slice: x: 4, y: 4, z: 8, core: 2. Of those that a mesh axis runs over, the one named last changes fastest.
Arguments:
- hidden: bfloat16 [65536, 8192], P('dp', 'fsdp'), may hold values from -50 to 50
- logit_grad: bfloat16 [65536, 1024], P('dp'), may hold values from -20 to 20
- master: float32 [1024, 8192], P('dp', 'fsdp'), may hold values from -6 to 6
- moment_one: float32 [1024, 8192], P('dp', 'fsdp'), may hold values from -4 to 4
- moment_two: float32 [1024, 8192], P('dp', 'fsdp'), may hold values from 0.25 to 4
Outputs:
- new_rows: bfloat16 [1024, 8192], P(None, 'fsdp')
- new_master: float32 [1024, 8192], P('dp', 'fsdp')
- new_one: float32 [1024, 8192], P('dp', 'fsdp')
- new_two: float32 [1024, 8192], P('dp', 'fsdp')
The draws below stay inside these ranges and needn't reach their ends.
All inputs are finite; a program needn't handle non-finite values.
Results may differ from the reference program's by a relative error of at most 0.012.
Values may be sent and summed in bfloat16 or wider, within the bound.
No kernel may reach another device: no remote copies, remote signals or barrier semaphores. Data moves between devices by JAX's collectives and lax.ppermute only.
A program may use at most 64 MiB of HBM per device.

```python
import math
import jax
import jax.numpy as jnp
from jax import lax

D = 8192
ROW_DEV = 32
TOK_DEV = 2048
ROWS = 1024
TOKENS = 65536


def token_sign(key):
    flips = jax.random.bernoulli(jax.random.fold_in(key, 41), 0.5, (TOKENS,))
    return jnp.where(flips, 1.0, -1.0).astype(jnp.float32)


def draw_hidden(key, part):
    key_col = jax.random.fold_in(key, 11)
    key_val = jax.random.fold_in(key, 12)
    key_dir = jax.random.fold_in(key, 14)
    column = jnp.arange(D, dtype=jnp.float32) / D
    colscale = 10.0 ** jax.random.uniform(key_col, (D,), jnp.float32)
    colscale = colscale * 3.0 ** column
    sign = token_sign(key)
    direction = jax.random.truncated_normal(key_dir, -2.0, 2.0, (D,), jnp.float32)
    values = jax.random.truncated_normal(key_val, -4.0, 4.0, (TOKENS, D), jnp.float32)
    amount = 0.69 * float(TOK_DEV) ** (-0.25)
    values = values + amount * sign[:, None] * direction[None, :]
    scaled = values * colscale[None, :] / 3.0
    return jnp.clip(scaled, -50.0, 50.0).astype(jnp.bfloat16)


def draw_logit_grad(key, part):
    key_row = jax.random.fold_in(key, 21)
    key_val = jax.random.fold_in(key, 22)
    key_dir = jax.random.fold_in(key, 25)
    key_cell = jax.random.fold_in(key, 26)
    blocks = TOKENS // TOK_DEV
    row_blocks = ROWS // ROW_DEV
    position = jnp.arange(ROWS, dtype=jnp.float32) / ROWS
    spread = 10.0 ** jax.random.uniform(key_row, (ROWS,), jnp.float32)
    values = jax.random.truncated_normal(key_val, -4.0, 4.0, (TOKENS, ROWS), jnp.float32)
    sign = token_sign(key)
    direction = jax.random.truncated_normal(key_dir, -2.0, 2.0, (ROWS,), jnp.float32)
    rising = 3.0 ** position
    amount = 0.69 * float(TOK_DEV) ** (-0.25)
    values = values + amount * sign[:, None] * direction[None, :]
    values = 0.006 * values * (rising * spread)[None, :]
    cell = 10.0 ** jax.random.uniform(key_cell, (blocks, row_blocks), jnp.float32, -1.0, 1.0)
    values = values.reshape(blocks, TOK_DEV, row_blocks, ROW_DEV) * cell[:, None, :, None]
    values = values.reshape(TOKENS, ROWS)
    return jnp.clip(values, -20.0, 20.0).astype(jnp.bfloat16)


def block_levels(key, extent, pieces, smallest, high):
    loudness, own = 1.0, jax.random.fold_in(key, 6)
    for dim, blocks in pieces:
        steps = jnp.exp(jax.random.uniform(jax.random.fold_in(own, dim), (blocks,), jnp.float32, smallest / len(pieces), high / len(pieces)))
        loudness = loudness * jnp.repeat(steps, extent[dim] // blocks).reshape([-1 if axis == dim else 1 for axis in range(len(extent))])
    return loudness


def noise(stream_key, dims, scale, bound, split=(), kind=jnp.bfloat16):
    values = jax.random.normal(stream_key, dims, jnp.float32) * scale
    if len(split) > 0:
        values = block_levels(stream_key, dims, split, -0.22, 0.18) * values
    return jnp.clip(values, min=-bound, max=bound).astype(kind)


def setup_inputs(seed: int = 0) -> dict:
    streams_of = jax.random.split(jax.random.key(seed), 6)
    hidden = draw_hidden(jax.random.fold_in(streams_of[5], 71), 0)
    logit_grad = draw_logit_grad(jax.random.fold_in(streams_of[5], 71), 0)
    master = noise(streams_of[2], (ROWS, D), 1.0, 6.0, ((0, 32), (1, 8)), jnp.float32)
    moment_one = noise(streams_of[3], (ROWS, D), 0.5, 4.0, ((0, 32), (1, 8)), jnp.float32)
    moment_two = jnp.clip(jnp.exp(math.log(4.0) - 2.7725887 * jax.random.uniform(streams_of[4], (ROWS, D), jnp.float32) ** block_levels(streams_of[4], (ROWS, D), ((0, 32), (1, 8)), -0.2, 0.2)), 0.25, 4.0)
    return dict(hidden=hidden, logit_grad=logit_grad, master=master, moment_one=moment_one, moment_two=moment_two)


def reference(hidden, logit_grad, master, moment_one, moment_two):
    blocks = TOKENS // TOK_DEV
    hid = hidden.reshape(blocks, TOK_DEV, D)
    lgr = logit_grad.reshape(blocks, TOK_DEV, ROWS)

    def accumulate(total, pair):
        states, grads = pair
        part = lax.dot_general(grads, states, (((0,), (0,)), ((), ())), preferred_element_type=jnp.float32)
        part = lax.optimization_barrier(part.astype(jnp.bfloat16)).astype(jnp.float32)
        return (total + part, None)
    grad, _ = lax.scan(accumulate, jnp.zeros((ROWS, D), jnp.float32), (hid, lgr))
    sumsq = jnp.sum(grad * grad)
    rms = jnp.sqrt(sumsq / (ROWS * D))
    factor = jnp.minimum(1.0, 1.0 / rms)
    clipped = factor * grad
    new_one = 0.9 * moment_one + 0.1 * clipped
    new_two = 0.95 * moment_two + 0.05 * clipped * clipped
    first = new_one / (1.0 - 0.9 ** 10)
    second = new_two / (1.0 - 0.95 ** 10)
    new_master = master - 0.05 * (first / (jnp.sqrt(second) + 1e-08) + 0.1 * master)
    return (new_master.astype(jnp.bfloat16), new_master, new_one, new_two)
```

```python
import jax
import jax.numpy as jnp
from jax import lax
from jax.sharding import Mesh
from jax.sharding import PartitionSpec as P

CHIPS = ("dp_0", "dp_1")
CORE = "dp_2"
DP = (*CHIPS, CORE)
SWAP = [(0, 1), (1, 0)]


def core_sums(logit_grad, hidden, chips, here):
    part = lax.dot_general(
        logit_grad, hidden, (((0,), (0,)), ((), ())), preferred_element_type=jnp.float32
    ).astype(jnp.bfloat16)
    blocks = part.reshape(chips, 2, -1, part.shape[1])
    kept = lax.dynamic_index_in_dim(blocks, here, 1, keepdims=False)
    sent = lax.dynamic_index_in_dim(blocks, 1 - here, 1, keepdims=False)
    return kept, lax.ppermute(sent, CORE, SWAP)


def added(pair):
    kept, arrived = pair
    return (kept.astype(jnp.float32) + arrived.astype(jnp.float32)).astype(jnp.bfloat16)


def shards(hidden, logit_grad, master, moment_one, moment_two):
    rows, columns = master.shape
    total_rows = logit_grad.shape[1]
    width = columns * lax.axis_size("fsdp")
    chips = lax.axis_size(CHIPS)
    everyone = (*DP, "fsdp")
    here = lax.axis_index(CORE)

    half = columns // 2
    pairs = [
        core_sums(logit_grad, hidden[:, start : start + half], chips, here)
        for start in (0, half)
    ]
    sums = jnp.concatenate([added(pair) for pair in pairs], axis=2)
    arrived = lax.all_to_all(sums, CHIPS, split_axis=0, concat_axis=0, tiled=True)
    grad = arrived.astype(jnp.float32).sum(axis=0)

    squares = (grad * grad).reshape(rows, columns // 128, 128).sum(axis=(0, 1))
    count = lax.axis_size(everyone)
    copies = jnp.broadcast_to(squares[None, None], (count, 1, 128))
    sumsq = jnp.sum(lax.all_to_all(copies, everyone, 0, 0, tiled=True))

    rms_value = jnp.sqrt(sumsq / (total_rows * width))
    factor = jnp.minimum(1.0, 1.0 / rms_value)
    clipped = factor * grad
    new_one = 0.9 * moment_one + 0.1 * clipped
    new_two = 0.95 * moment_two + 0.05 * clipped * clipped
    first = new_one / (1.0 - 0.9**10)
    second = new_two / (1.0 - 0.95**10)
    new_master = master - 0.05 * (first / (jnp.sqrt(second) + 1e-08) + 0.1 * master)
    own_rows = new_master.astype(jnp.bfloat16)

    spread = jnp.broadcast_to(own_rows[None], (chips, rows, columns))
    mine = lax.all_to_all(spread, CHIPS, 0, 0, tiled=True)
    other = lax.ppermute(mine, CORE, SWAP)
    even = jnp.where(here == 0, mine, other)
    odd = jnp.where(here == 0, other, mine)
    new_rows = jnp.stack([even, odd], axis=1).reshape(total_rows, columns)
    return (new_rows, new_master, new_one, new_two)


def solution(mesh):
    torus = Mesh(mesh.devices.reshape(4, 4, 2, mesh.shape["fsdp"]), (*DP, "fsdp"))
    placed = (P(DP, "fsdp"), P(DP, None), P(DP, "fsdp"), P(DP, "fsdp"), P(DP, "fsdp"))
    return jax.shard_map(
        shards,
        mesh=torus,
        in_specs=placed,
        out_specs=(P(None, "fsdp"), P(DP, "fsdp"), P(DP, "fsdp"), P(DP, "fsdp")),
        check_vma=False,
    )
```

```python
import functools

import jax
import jax.numpy as jnp
from jax import lax
from jax.experimental import pallas as pl
from jax.experimental.pallas import tpu as pltpu
from jax.sharding import Mesh
from jax.sharding import PartitionSpec as P

CHIPS = ("dp_0", "dp_1")
CORE = "dp_2"
DP = (*CHIPS, CORE)
SIDE = 4
SWAP = [(0, 1), (1, 0)]
VMEM = pl.BlockSpec(memory_space=pltpu.VMEM)
HBM = pl.BlockSpec(memory_space=pl.ANY)
BF16, F32 = jnp.bfloat16, jnp.float32


def near(value):
    return pltpu.with_memory_space_constraint(value, pltpu.VMEM)


def far(value):
    return pltpu.with_memory_space_constraint(value, pltpu.HBM)


def call(body, outs, args, flops=0, moved=0, specs=None, out_specs=None, **more):
    return pl.pallas_call(
        body,
        out_shape=outs,
        in_specs=specs or [VMEM] * len(args),
        out_specs=out_specs or [VMEM] * len(outs),
        cost_estimate=pl.CostEstimate(flops=flops, bytes_accessed=moved, transcendentals=0),
        compiler_params=pltpu.CompilerParams(vmem_limit_bytes=24 * 2**20),
        **more,
    )(*args)


def product(left, right):
    return lax.dot_general(left, right, (((0,), (0,)), ((), ())), preferred_element_type=F32)


def load_and_multiply(chunks, lanes, lg_hbm, hid_hbm, lg, mine, sent, theirs, total, sems):
    here = lax.axis_index(CORE)
    tokens, rows = lg.shape
    half = mine.shape[1]
    step = tokens // chunks
    own = pl.ds(pl.multiple_of(here * half, half), half)
    other = pl.ds(pl.multiple_of((1 - here) * half, half), half)
    copies = []
    for k in range(chunks):
        part = pl.ds(k * step, step)
        copies.append(
            (
                pltpu.make_async_copy(lg_hbm.at[part], lg.at[part], sems.at[k, 0]),
                pltpu.make_async_copy(hid_hbm.at[part, other], theirs.at[part], sems.at[k, 1]),
            )
        )
        for copy in copies[-1]:
            copy.start()
    last = pltpu.make_async_copy(hid_hbm.at[:, own], mine, sems.at[chunks, 0])
    last.start()
    for k in range(chunks):
        part = pl.ds(k * step, step)
        for copy in copies[k]:
            copy.wait()
        for first in range(0, rows, lanes):
            block = pl.ds(first, lanes)
            value = product(lg[part, block], theirs[part, :])
            if k > 0:
                value += total[block, :]
            if k < chunks - 1:
                total[block, :] = value
            else:
                sent[block, :] = value.astype(BF16)
    last.wait()


def multiply(lanes, lg, hid, out):
    for first in range(0, lg.shape[1], lanes):
        block = pl.ds(first, lanes)
        out[block, :] = product(lg[:, block], hid[...]).astype(BF16)


def arrange(kept, arrived, *outs):
    here, row, column = (lax.axis_index(axis) for axis in (CORE, *CHIPS))
    size = outs[0].shape[1]
    for mask, out in enumerate(outs):
        for place in range(SIDE):
            block = jnp.where(
                here == 0,
                place * SIDE + lax.bitwise_xor(column, mask),
                lax.bitwise_xor(row, mask) * SIDE + place,
            )
            rows = pl.ds(pl.multiple_of(block * size, size), size)
            out[place] = (kept[rows, :].astype(F32) + arrived[rows, :].astype(F32)).astype(BF16)


def add_first(own, one, two, three, *outs):
    here, row, column = (lax.axis_index(axis) for axis in (CORE, *CHIPS))
    second = jnp.where(here == 0, row, column)
    for mask, out in enumerate(outs):
        place = lax.bitwise_xor(second, mask)
        total = own[place].astype(F32) + one[place].astype(F32)
        total += two[place].astype(F32) + three[place].astype(F32)
        out[...] = total.astype(out.dtype)


def add_second(own, one, two, three, kept, sent, squares, grad):
    here = lax.axis_index(CORE)
    rows, columns = kept.shape
    value = own[...] + one[...].astype(F32) + two[...].astype(F32) + three[...].astype(F32)
    grad[...] = value
    square = value * value
    lanes = sum(square[:, first : first + 128] for first in range(0, columns, 128))
    squares[...] = jnp.sum(lanes, axis=0, keepdims=True)
    kept[...] = grad[pl.ds(pl.multiple_of(here * rows, rows), rows), :]
    sent[...] = grad[pl.ds(pl.multiple_of((1 - here) * rows, rows), rows), :]


def update(entries, sums, kept, arrived, master, moment_one, moment_two, *outs):
    spread, new_master, new_one, new_two = outs
    here = lax.axis_index(CORE)
    half = kept.shape[1]
    sumsq = jnp.sum(jnp.sum(sums[...], axis=0, keepdims=True), axis=1, keepdims=True)
    factor = jnp.minimum(1.0, 1.0 / jnp.sqrt(sumsq / entries))
    for place, part in ((here, kept), (1 - here, arrived)):
        columns = pl.ds(pl.multiple_of(place * half, half), half)
        clipped = factor * part[...]
        one = 0.9 * moment_one[:, columns] + 0.1 * clipped
        two = 0.95 * moment_two[:, columns] + 0.05 * clipped * clipped
        first = one / (1.0 - 0.9**10)
        second = two / (1.0 - 0.95**10)
        old = master[:, columns]
        value = old - 0.05 * (first / (jnp.sqrt(second) + 1e-08) + 0.1 * old)
        new_one[:, columns] = one
        new_two[:, columns] = two
        new_master[:, columns] = value
        for chip in range(spread.shape[0]):
            spread[chip, :, columns] = value.astype(BF16)


def write_own(mine, out, sem):
    copy = pltpu.make_async_copy(mine, out.at[:, lax.axis_index(CORE)], sem)
    copy.start()
    copy.wait()


def write_other(other, written, out, sem):
    del written
    copy = pltpu.make_async_copy(other, out.at[:, 1 - lax.axis_index(CORE)], sem)
    copy.start()
    copy.wait()


def partners(mask, stage):
    pairs = []
    for row in range(SIDE):
        for column in range(SIDE):
            for core in range(2):
                place = (row * SIDE + column) * 2 + core
                if core == stage:
                    other = (row * SIDE + (column ^ mask)) * 2 + core
                else:
                    other = ((row ^ mask) * SIDE + column) * 2 + core
                pairs.append((place, other))
    return pairs


def shards(hidden, logit_grad, master, moment_one, moment_two):
    rows, columns = master.shape
    tokens, total_rows = logit_grad.shape
    half = columns // 2
    chips = SIDE * SIDE
    everyone = (*DP, "fsdp")
    count = lax.axis_size(everyone)
    width = columns * lax.axis_size("fsdp")
    work = 2 * tokens * total_rows * half

    chunks = 4
    lg, hid, sent = call(
        functools.partial(load_and_multiply, chunks, 256),
        [
            pltpu.VMEM((tokens, total_rows), BF16),
            pltpu.VMEM((tokens, half), BF16),
            pltpu.VMEM((total_rows, half), BF16),
        ],
        [far(logit_grad), far(hidden)],
        flops=work,
        moved=4 * tokens * columns,
        specs=[HBM, HBM],
        scratch_shapes=[
            pltpu.VMEM((tokens, half), BF16),
            pltpu.VMEM((total_rows, half), F32),
            pltpu.SemaphoreType.DMA((chunks + 1, 2)),
        ],
    )
    arrived = lax.ppermute(sent, CORE, SWAP)
    (kept,) = call(
        functools.partial(multiply, 256),
        [pltpu.VMEM((total_rows, half), BF16)],
        [near(lg), near(hid)],
        flops=work,
        moved=tokens * columns,
    )
    blocks = call(
        arrange,
        [pltpu.VMEM((SIDE, 2 * rows, half), BF16)] * SIDE,
        [near(kept), near(arrived)],
    )
    first = [blocks[0]] + [
        lax.ppermute(blocks[mask], DP, partners(mask, 0)) for mask in range(1, SIDE)
    ]
    totals = call(
        add_first,
        [pltpu.VMEM((2 * rows, half), F32)] + [pltpu.VMEM((2 * rows, half), BF16)] * (SIDE - 1),
        [near(value) for value in first],
    )
    second = [totals[0]] + [
        lax.ppermute(totals[mask], DP, partners(mask, 1)) for mask in range(1, SIDE)
    ]
    grad_here, grad_sent, squares = call(
        add_second,
        [pltpu.VMEM((rows, half), F32)] * 2 + [pltpu.VMEM((1, 128), F32)],
        [near(value) for value in second],
        scratch_shapes=[pltpu.VMEM((2 * rows, half), F32)],
    )
    grad_there = lax.ppermute(grad_sent, CORE, SWAP)
    copies = jnp.broadcast_to(squares[None], (count, 1, 128))
    sums = lax.all_to_all(copies, everyone, 0, 0, tiled=True).reshape(count, 128)

    spread, new_master, new_one, new_two = call(
        functools.partial(update, float(total_rows * width)),
        [pltpu.VMEM((chips, rows, columns), BF16)] + [pltpu.VMEM((rows, columns), F32)] * 3,
        [near(v) for v in (sums, grad_here, grad_there, master, moment_one, moment_two)],
    )
    mine = lax.all_to_all(spread, CHIPS, 0, 0, tiled=True)
    other = lax.ppermute(mine, CORE, SWAP)
    (written,) = call(
        write_own,
        [pltpu.HBM((chips, 2, rows, columns), BF16)],
        [near(mine)],
        moved=total_rows * columns * 2,
        out_specs=[HBM],
        scratch_shapes=[pltpu.SemaphoreType.DMA],
    )
    (new_rows,) = call(
        write_other,
        [pltpu.HBM((chips, 2, rows, columns), BF16)],
        [near(other), far(written)],
        moved=total_rows * columns * 2,
        specs=[VMEM, HBM],
        out_specs=[HBM],
        scratch_shapes=[pltpu.SemaphoreType.DMA],
        input_output_aliases={1: 0},
    )
    return (new_rows.reshape(total_rows, columns), new_master, new_one, new_two)


def solution(mesh):
    torus = Mesh(
        mesh.devices.reshape(SIDE, SIDE, 2, mesh.shape["fsdp"]), (*DP, "fsdp")
    )
    placed = (P(DP, "fsdp"), P(DP, None), P(DP, "fsdp"), P(DP, "fsdp"), P(DP, "fsdp"))
    return jax.shard_map(
        shards,
        mesh=torus,
        in_specs=placed,
        out_specs=(P(None, "fsdp"), P(DP, "fsdp"), P(DP, "fsdp"), P(DP, "fsdp")),
        check_vma=False,
    )
```

```python
import functools

import jax
import jax.numpy as jnp
from jax import lax
from jax.experimental import pallas as pl
from jax.experimental.pallas import tpu as pltpu
from jax.sharding import Mesh
from jax.sharding import PartitionSpec as P

CHIPS = ("dp_0", "dp_1")
CORE = "dp_2"
DP = (*CHIPS, CORE)
SIDE = 4
SWAP = [(0, 1), (1, 0)]
VMEM = pl.BlockSpec(memory_space=pltpu.VMEM)
HBM = pl.BlockSpec(memory_space=pl.ANY)
BF16, F32 = jnp.bfloat16, jnp.float32


def near(value):
    return pltpu.with_memory_space_constraint(value, pltpu.VMEM)


def far(value):
    return pltpu.with_memory_space_constraint(value, pltpu.HBM)


def call(body, outs, args, flops=0, moved=0, specs=None, out_specs=None, **more):
    return pl.pallas_call(
        body,
        out_shape=outs,
        in_specs=specs or [VMEM] * len(args),
        out_specs=out_specs or [VMEM] * len(outs),
        cost_estimate=pl.CostEstimate(flops=flops, bytes_accessed=moved, transcendentals=0),
        compiler_params=pltpu.CompilerParams(vmem_limit_bytes=24 * 2**20),
        **more,
    )(*args)


def product(left, right):
    return lax.dot_general(left, right, (((0,), (0,)), ((), ())), preferred_element_type=F32)


def core_columns(half):
    here = lax.axis_index(CORE)
    own = pl.ds(pl.multiple_of(here * half, half), half)
    return own, pl.ds(pl.multiple_of((1 - here) * half, half), half)


def load_and_multiply(chunks, lanes, lg_hbm, hid_hbm, lg, mine, sent, theirs, total, sems):
    tokens, rows = lg.shape
    step = tokens // chunks
    own, other = core_columns(mine.shape[1])
    copies = []
    for k in range(chunks):
        part = pl.ds(k * step, step)
        copies.append(
            (
                pltpu.make_async_copy(lg_hbm.at[part], lg.at[part], sems.at[k, 0]),
                pltpu.make_async_copy(hid_hbm.at[part, other], theirs.at[part], sems.at[k, 1]),
            )
        )
        for copy in copies[-1]:
            copy.start()
    last = pltpu.make_async_copy(
        hid_hbm.at[:, own], mine, sems.at[chunks, 0]
    )
    last.start()
    for k in range(chunks):
        part = pl.ds(k * step, step)
        for copy in copies[k]:
            copy.wait()
        for first in range(0, rows, lanes):
            block = pl.ds(first, lanes)
            value = product(lg[part, block], theirs[part, :])
            if k > 0:
                value += total[block, :]
            if k < chunks - 1:
                total[block, :] = value
            else:
                sent[block, :] = value.astype(BF16)
    last.wait()


def multiply(lanes, lg, hid, out):
    for first in range(0, lg.shape[1], lanes):
        block = pl.ds(first, lanes)
        out[block, :] = product(lg[:, block], hid[...]).astype(BF16)


def arrange(kept, arrived, *outs):
    here, row, column = (lax.axis_index(axis) for axis in (CORE, *CHIPS))
    size = outs[0].shape[1]
    for mask, out in enumerate(outs):
        for place in range(SIDE):
            block = jnp.where(
                here == 0,
                place * SIDE + lax.bitwise_xor(column, mask),
                lax.bitwise_xor(row, mask) * SIDE + place,
            )
            rows = pl.ds(pl.multiple_of(block * size, size), size)
            out[place] = (kept[rows, :].astype(F32) + arrived[rows, :].astype(F32)).astype(BF16)


def add_first(own, one, two, three, *outs):
    here, row, column = (lax.axis_index(axis) for axis in (CORE, *CHIPS))
    second = jnp.where(here == 0, row, column)
    for mask, out in enumerate(outs):
        place = lax.bitwise_xor(second, mask)
        total = own[place].astype(F32) + one[place].astype(F32)
        total += two[place].astype(F32) + three[place].astype(F32)
        out[...] = total.astype(out.dtype)


def add_second(own, one, two, three, grad, squares):
    value = own[...] + one[...].astype(F32) + two[...].astype(F32) + three[...].astype(F32)
    grad[...] = value
    square = value * value
    lanes = sum(square[:, first : first + 128] for first in range(0, value.shape[1], 128))
    squares[...] = jnp.broadcast_to(jnp.sum(lanes, axis=0, keepdims=True)[None], squares.shape)


def pack(*refs):
    (*sources, out) = refs
    _, other = core_columns(out.shape[2])
    for number, source in enumerate(sources):
        out[number] = source[:, other]


def update(entries, sums, grad, master, moment_one, moment_two, packed, values, kept, sent):
    here = lax.axis_index(CORE)
    rows, half = kept.shape[1:]
    own, _ = core_columns(half)
    sumsq = jnp.sum(jnp.sum(sums[...], axis=0, keepdims=True), axis=1, keepdims=True)
    factor = jnp.minimum(1.0, 1.0 / jnp.sqrt(sumsq / entries))
    owned = (master[:, own], moment_one[:, own], moment_two[:, own])
    lent = (packed[0], packed[1], packed[2])
    for core, (old, old_one, old_two), out in ((here, owned, kept), (1 - here, lent, sent)):
        place = pl.ds(pl.multiple_of(core * rows, rows), rows)
        clipped = factor * grad[place, :]
        one = 0.9 * old_one + 0.1 * clipped
        two = 0.95 * old_two + 0.05 * clipped * clipped
        first = one / (1.0 - 0.9**10)
        second = two / (1.0 - 0.95**10)
        value = old - 0.05 * (first / (jnp.sqrt(second) + 1e-08) + 0.1 * old)
        out[0], out[1], out[2] = value, one, two
        values[place, :] = value.astype(BF16)


def join(*refs):
    (*sources, out) = refs
    for number, source in enumerate(sources):
        out[number] = source[...]


def row_copies(source, second_mask, core, out, sems, number):
    row, column = (lax.axis_index(axis) for axis in CHIPS)
    size, half = source.shape[1:]
    columns = pl.ds(pl.multiple_of(core * half, half), half)
    copies = []
    for mask in range(SIDE):
        chip = jnp.where(
            core == 0,
            lax.bitwise_xor(row, mask) * SIDE + lax.bitwise_xor(column, second_mask),
            lax.bitwise_xor(row, second_mask) * SIDE + lax.bitwise_xor(column, mask),
        )
        rows = pl.ds(pl.multiple_of(chip * size, size), size)
        copies.append(
            pltpu.make_async_copy(source.at[mask], out.at[rows, columns], sems.at[number + mask])
        )
    return copies


def write_early(*refs):
    (*own, arrived, kept, given, out, new_master, new_one, new_two, sems) = refs
    here = lax.axis_index(CORE)
    copies = []
    for mask, source in enumerate(own):
        copies += row_copies(source, mask, here, out, sems, len(copies))
    copies += row_copies(arrived, 0, 1 - here, out, sems, len(copies))
    for source, columns in zip((kept, given), core_columns(kept.shape[2])):
        for number, target in enumerate((new_master, new_one, new_two)):
            copies.append(
                pltpu.make_async_copy(
                    source.at[number], target.at[:, columns], sems.at[len(copies)]
                )
            )
    for copy in copies:
        copy.start()
    for copy in copies:
        copy.wait()


def write_late(*refs):
    (*arrived, _, out, sems) = refs
    here = lax.axis_index(CORE)
    copies = []
    for mask, source in enumerate(arrived, 1):
        copies += row_copies(source, mask, 1 - here, out, sems, len(copies))
    for copy in copies:
        copy.start()
    for copy in copies:
        copy.wait()


def partners(mask, stage):
    pairs = []
    for row in range(SIDE):
        for column in range(SIDE):
            for core in range(2):
                place = (row * SIDE + column) * 2 + core
                if core == stage:
                    other = (row * SIDE + (column ^ mask)) * 2 + core
                else:
                    other = ((row ^ mask) * SIDE + column) * 2 + core
                pairs.append((place, other))
    return pairs


def shards(hidden, logit_grad, master, moment_one, moment_two):
    rows, columns = master.shape
    tokens, total_rows = logit_grad.shape
    half = columns // 2
    everyone = (*DP, "fsdp")
    count = lax.axis_size(everyone)
    width = columns * lax.axis_size("fsdp")
    work = 2 * tokens * total_rows * half

    chunks = 4
    lg, mine, sent = call(
        functools.partial(load_and_multiply, chunks, 256),
        [
            pltpu.VMEM((tokens, total_rows), BF16),
            pltpu.VMEM((tokens, half), BF16),
            pltpu.VMEM((total_rows, half), BF16),
        ],
        [far(logit_grad), far(hidden)],
        flops=work,
        moved=4 * tokens * columns,
        specs=[HBM, HBM],
        scratch_shapes=[
            pltpu.VMEM((tokens, half), BF16),
            pltpu.VMEM((total_rows, half), F32),
            pltpu.SemaphoreType.DMA((chunks + 1, 2)),
        ],
    )
    arrived = lax.ppermute(sent, CORE, SWAP)
    (kept,) = call(
        functools.partial(multiply, 256),
        [pltpu.VMEM((total_rows, half), BF16)],
        [near(lg), near(mine)],
        flops=work,
        moved=tokens * columns,
    )
    blocks = call(
        arrange,
        [pltpu.VMEM((SIDE, 2 * rows, half), BF16)] * SIDE,
        [near(kept), near(arrived)],
    )
    first = [blocks[0]] + [
        lax.ppermute(blocks[mask], DP, partners(mask, 0)) for mask in range(1, SIDE)
    ]
    *states, _ = lax.optimization_barrier((master, moment_one, moment_two, first[1]))
    (lent,) = call(
        pack, [pltpu.VMEM((3, rows, half), F32)], [near(state) for state in states]
    )
    packed = lax.ppermute(lent, CORE, SWAP)
    totals = call(
        add_first,
        [pltpu.VMEM((2 * rows, half), F32)] + [pltpu.VMEM((2 * rows, half), BF16)] * (SIDE - 1),
        [near(value) for value in first],
    )
    second = [totals[0]] + [
        lax.ppermute(totals[mask], DP, partners(mask, 1)) for mask in range(1, SIDE)
    ]
    grad, copies = call(
        add_second,
        [pltpu.VMEM((2 * rows, half), F32), pltpu.VMEM((count, 1, 128), F32)],
        [near(value) for value in second],
    )
    copies, packed = lax.optimization_barrier((copies, packed))
    sums = lax.all_to_all(copies, everyone, 0, 0, tiled=True).reshape(count, 128)

    values, kept, sent = call(
        functools.partial(update, float(total_rows * width)),
        [pltpu.VMEM((2 * rows, half), BF16)] + [pltpu.VMEM((3, rows, half), F32)] * 2,
        [near(value) for value in (sums, grad, *states, packed)],
    )
    line = [values] + [lax.ppermute(values, DP, partners(mask, 1)) for mask in range(1, SIDE)]
    (joined,) = call(
        join, [pltpu.VMEM((SIDE, 2 * rows, half), BF16)], [near(value) for value in line]
    )
    given = lax.ppermute(sent, CORE, SWAP)
    plane = [joined] + [lax.ppermute(joined, DP, partners(mask, 0)) for mask in range(1, SIDE)]
    plane[1], given = lax.optimization_barrier((plane[1], given))
    others = [lax.ppermute(value, CORE, SWAP) for value in plane]
    slab = pltpu.HBM((total_rows, columns), BF16)
    written, new_master, new_one, new_two = call(
        write_early,
        [slab] + [pltpu.HBM((rows, columns), F32)] * 3,
        [near(value) for value in (*plane, others[0], kept, given)],
        moved=total_rows * columns * 2,
        out_specs=[HBM] * 4,
        scratch_shapes=[pltpu.SemaphoreType.DMA((SIDE * (SIDE + 1) + 6,))],
    )
    (new_rows,) = call(
        write_late,
        [slab],
        [*(near(value) for value in others[1:]), far(written)],
        moved=total_rows * columns * 2,
        specs=[VMEM] * (SIDE - 1) + [HBM],
        out_specs=[HBM],
        scratch_shapes=[pltpu.SemaphoreType.DMA((SIDE * (SIDE - 1),))],
        input_output_aliases={SIDE - 1: 0},
    )
    return (new_rows, new_master, new_one, new_two)


def solution(mesh):
    torus = Mesh(
        mesh.devices.reshape(SIDE, SIDE, 2, mesh.shape["fsdp"]), (*DP, "fsdp")
    )
    placed = (P(DP, "fsdp"), P(DP, None), P(DP, "fsdp"), P(DP, "fsdp"), P(DP, "fsdp"))
    return jax.shard_map(
        shards,
        mesh=torus,
        in_specs=placed,
        out_specs=(P(None, "fsdp"), P(DP, "fsdp"), P(DP, "fsdp"), P(DP, "fsdp")),
        check_vma=False,
    )
```

```python
import functools

import jax
import jax.numpy as jnp
from jax import lax
from jax.experimental import pallas as pl
from jax.experimental.pallas import tpu as pltpu
from jax.sharding import Mesh
from jax.sharding import PartitionSpec as P

CHIPS = ("dp_0", "dp_1")
CORE = "dp_2"
DP = (*CHIPS, CORE)
SIDE = 4
SWAP = [(0, 1), (1, 0)]
VMEM = pl.BlockSpec(memory_space=pltpu.VMEM)
HBM = pl.BlockSpec(memory_space=pl.ANY)
BF16, F32 = jnp.bfloat16, jnp.float32


def near(value):
    return pltpu.with_memory_space_constraint(value, pltpu.VMEM)


def far(value):
    return pltpu.with_memory_space_constraint(value, pltpu.HBM)


def call(body, outs, args, flops=0, moved=0, specs=None, out_specs=None, **more):
    return pl.pallas_call(
        body,
        out_shape=outs,
        in_specs=specs or [VMEM] * len(args),
        out_specs=out_specs or [VMEM] * len(outs),
        cost_estimate=pl.CostEstimate(flops=flops, bytes_accessed=moved, transcendentals=0),
        compiler_params=pltpu.CompilerParams(vmem_limit_bytes=24 * 2**20),
        **more,
    )(*args)


def product(left, right):
    return lax.dot_general(left, right, (((0,), (0,)), ((), ())), preferred_element_type=F32)


def core_columns(half):
    here = lax.axis_index(CORE)
    own = pl.ds(pl.multiple_of(here * half, half), half)
    return own, pl.ds(pl.multiple_of((1 - here) * half, half), half)


def load_and_multiply(chunks, lanes, lg_hbm, hid_hbm, lg, mine, sent, theirs, total, sems):
    tokens, rows = lg.shape
    step = tokens // chunks
    own, other = core_columns(mine.shape[1])
    copies = []
    for k in range(chunks):
        part = pl.ds(k * step, step)
        copies.append(
            (
                pltpu.make_async_copy(lg_hbm.at[part], lg.at[part], sems.at[k, 0]),
                pltpu.make_async_copy(hid_hbm.at[part, other], theirs.at[part], sems.at[k, 1]),
            )
        )
        for copy in copies[-1]:
            copy.start()
    last = pltpu.make_async_copy(
        hid_hbm.at[:, own], mine, sems.at[chunks, 0]
    )
    last.start()
    for k in range(chunks):
        part = pl.ds(k * step, step)
        for copy in copies[k]:
            copy.wait()
        for first in range(0, rows, lanes):
            block = pl.ds(first, lanes)
            value = product(lg[part, block], theirs[part, :])
            if k > 0:
                value += total[block, :]
            if k < chunks - 1:
                total[block, :] = value
            else:
                sent[block, :] = value.astype(BF16)
    last.wait()


def multiply(lanes, lg, hid, out):
    for first in range(0, lg.shape[1], lanes):
        block = pl.ds(first, lanes)
        out[block, :] = product(lg[:, block], hid[...]).astype(BF16)


def arrange(kept, arrived, *outs):
    here, row, column = (lax.axis_index(axis) for axis in (CORE, *CHIPS))
    size = outs[0].shape[1]
    for mask, out in enumerate(outs):
        for place in range(SIDE):
            block = jnp.where(
                here == 0,
                place * SIDE + lax.bitwise_xor(column, mask),
                lax.bitwise_xor(row, mask) * SIDE + place,
            )
            rows = pl.ds(pl.multiple_of(block * size, size), size)
            out[place] = (kept[rows, :].astype(F32) + arrived[rows, :].astype(F32)).astype(BF16)


def add_first(own, one, two, three, *outs):
    here, row, column = (lax.axis_index(axis) for axis in (CORE, *CHIPS))
    second = jnp.where(here == 0, row, column)
    for mask, out in enumerate(outs):
        place = lax.bitwise_xor(second, mask)
        total = own[place].astype(F32) + one[place].astype(F32)
        total += two[place].astype(F32) + three[place].astype(F32)
        out[...] = total.astype(out.dtype)


def add_second(own, one, two, three, grad, squares):
    value = own[...] + one[...].astype(F32) + two[...].astype(F32) + three[...].astype(F32)
    grad[...] = value
    square = value * value
    lanes = sum(square[:, first : first + 128] for first in range(0, value.shape[1], 128))
    squares[...] = jnp.broadcast_to(jnp.sum(lanes, axis=0, keepdims=True)[None], squares.shape)


def pack(*refs):
    (*sources, out) = refs
    _, other = core_columns(out.shape[2])
    for number, source in enumerate(sources):
        out[number] = source[:, other]


def update(entries, sums, grad, master, moment_one, moment_two, packed, values, kept, sent):
    here = lax.axis_index(CORE)
    rows, half = kept.shape[1:]
    own, _ = core_columns(half)
    sumsq = jnp.sum(jnp.sum(sums[...], axis=0, keepdims=True), axis=1, keepdims=True)
    factor = jnp.minimum(1.0, 1.0 / jnp.sqrt(sumsq / entries))
    owned = (master[:, own], moment_one[:, own], moment_two[:, own])
    lent = (packed[0], packed[1], packed[2])
    for core, (old, old_one, old_two), out in ((here, owned, kept), (1 - here, lent, sent)):
        place = pl.ds(pl.multiple_of(core * rows, rows), rows)
        clipped = factor * grad[place, :]
        one = 0.9 * old_one + 0.1 * clipped
        two = 0.95 * old_two + 0.05 * clipped * clipped
        first = one / (1.0 - 0.9**10)
        second = two / (1.0 - 0.95**10)
        value = old - 0.05 * (first / (jnp.sqrt(second) + 1e-08) + 0.1 * old)
        out[0], out[1], out[2] = value, one, two
        values[place, :] = value.astype(BF16)


def join(*refs):
    (*sources, out) = refs
    for number, source in enumerate(sources):
        out[number] = source[...]


def row_copies(source, second_mask, core, out, sems, number):
    row, column = (lax.axis_index(axis) for axis in CHIPS)
    size, half = source.shape[1:]
    columns = pl.ds(pl.multiple_of(core * half, half), half)
    copies = []
    for mask in range(SIDE):
        chip = jnp.where(
            core == 0,
            lax.bitwise_xor(row, mask) * SIDE + lax.bitwise_xor(column, second_mask),
            lax.bitwise_xor(row, second_mask) * SIDE + lax.bitwise_xor(column, mask),
        )
        rows = pl.ds(pl.multiple_of(chip * size, size), size)
        copies.append(
            pltpu.make_async_copy(source.at[mask], out.at[rows, columns], sems.at[number + mask])
        )
    return copies


def write_first(own, arrived, kept, given, out, new_master, new_one, new_two, sems):
    here = lax.axis_index(CORE)
    copies = row_copies(own, 0, here, out, sems, 0)
    copies += row_copies(arrived, 0, 1 - here, out, sems, len(copies))
    for source, columns in zip((kept, given), core_columns(kept.shape[2])):
        for number, target in enumerate((new_master, new_one, new_two)):
            copies.append(
                pltpu.make_async_copy(
                    source.at[number], target.at[:, columns], sems.at[len(copies)]
                )
            )
    for copy in copies:
        copy.start()
    for copy in copies:
        copy.wait()


def write_rest(other, *refs):
    (*sources, _, out, sems) = refs
    here = lax.axis_index(CORE)
    core = 1 - here if other else here
    copies = []
    for mask, source in enumerate(sources, 1):
        copies += row_copies(source, mask, core, out, sems, len(copies))
    for copy in copies:
        copy.start()
    for copy in copies:
        copy.wait()


def partners(mask, stage):
    pairs = []
    for row in range(SIDE):
        for column in range(SIDE):
            for core in range(2):
                place = (row * SIDE + column) * 2 + core
                if core == stage:
                    other = (row * SIDE + (column ^ mask)) * 2 + core
                else:
                    other = ((row ^ mask) * SIDE + column) * 2 + core
                pairs.append((place, other))
    return pairs


def shards(hidden, logit_grad, master, moment_one, moment_two):
    rows, columns = master.shape
    tokens, total_rows = logit_grad.shape
    half = columns // 2
    everyone = (*DP, "fsdp")
    count = lax.axis_size(everyone)
    width = columns * lax.axis_size("fsdp")
    work = 2 * tokens * total_rows * half

    chunks = 4
    lg, mine, sent = call(
        functools.partial(load_and_multiply, chunks, 256),
        [
            pltpu.VMEM((tokens, total_rows), BF16),
            pltpu.VMEM((tokens, half), BF16),
            pltpu.VMEM((total_rows, half), BF16),
        ],
        [far(logit_grad), far(hidden)],
        flops=work,
        moved=4 * tokens * columns,
        specs=[HBM, HBM],
        scratch_shapes=[
            pltpu.VMEM((tokens, half), BF16),
            pltpu.VMEM((total_rows, half), F32),
            pltpu.SemaphoreType.DMA((chunks + 1, 2)),
        ],
    )
    arrived = lax.ppermute(sent, CORE, SWAP)
    (kept,) = call(
        functools.partial(multiply, 256),
        [pltpu.VMEM((total_rows, half), BF16)],
        [near(lg), near(mine)],
        flops=work,
        moved=tokens * columns,
    )
    blocks = call(
        arrange,
        [pltpu.VMEM((SIDE, 2 * rows, half), BF16)] * SIDE,
        [near(kept), near(arrived)],
    )
    first = [blocks[0]] + [
        lax.ppermute(blocks[mask], DP, partners(mask, 0)) for mask in (2, 1, 3)
    ]
    *states, _ = lax.optimization_barrier((master, moment_one, moment_two, first[1]))
    (lent,) = call(
        pack, [pltpu.VMEM((3, rows, half), F32)], [near(state) for state in states]
    )
    packed = lax.ppermute(lent, CORE, SWAP)
    totals = call(
        add_first,
        [pltpu.VMEM((2 * rows, half), F32)] + [pltpu.VMEM((2 * rows, half), BF16)] * (SIDE - 1),
        [near(value) for value in first],
    )
    second = [totals[0]] + [
        lax.ppermute(totals[mask], DP, partners(mask, 1)) for mask in (2, 1, 3)
    ]
    grad, copies = call(
        add_second,
        [pltpu.VMEM((2 * rows, half), F32), pltpu.VMEM((count, 1, 128), F32)],
        [near(value) for value in second],
    )
    copies, packed = lax.optimization_barrier((copies, packed))
    sums = lax.all_to_all(copies, everyone, 0, 0, tiled=True).reshape(count, 128)

    values, kept, sent = call(
        functools.partial(update, float(total_rows * width)),
        [pltpu.VMEM((2 * rows, half), BF16)] + [pltpu.VMEM((3, rows, half), F32)] * 2,
        [near(value) for value in (sums, grad, *states, packed)],
    )
    line = {mask: lax.ppermute(values, DP, partners(mask, 1)) for mask in (1, 3, 2)}
    line = [values] + [line[mask] for mask in range(1, SIDE)]
    (joined,) = call(
        join, [pltpu.VMEM((SIDE, 2 * rows, half), BF16)], [near(value) for value in line]
    )
    given = lax.ppermute(sent, CORE, SWAP)
    plane = {mask: lax.ppermute(joined, DP, partners(mask, 0)) for mask in (1, 3, 2)}
    plane = [joined] + [plane[mask] for mask in range(1, SIDE)]
    plane[2], given = lax.optimization_barrier((plane[2], given))
    across = lax.ppermute(joined, CORE, SWAP)
    slab = pltpu.HBM((total_rows, columns), BF16)
    new_rows, new_master, new_one, new_two = call(
        write_first,
        [slab] + [pltpu.HBM((rows, columns), F32)] * 3,
        [near(value) for value in (joined, across, kept, given)],
        moved=total_rows * columns,
        out_specs=[HBM] * 4,
        scratch_shapes=[pltpu.SemaphoreType.DMA((2 * SIDE + 6,))],
    )
    plane[1], new_rows = lax.optimization_barrier((plane[1], new_rows))
    others = [lax.ppermute(value, CORE, SWAP) for value in plane[1:]]
    for other, sources in enumerate((plane[1:], others)):
        (new_rows,) = call(
            functools.partial(write_rest, other),
            [slab],
            [*(near(value) for value in sources), far(new_rows)],
            moved=total_rows * columns,
            specs=[VMEM] * (SIDE - 1) + [HBM],
            out_specs=[HBM],
            scratch_shapes=[pltpu.SemaphoreType.DMA((SIDE * (SIDE - 1),))],
            input_output_aliases={SIDE - 1: 0},
        )
    return (new_rows, new_master, new_one, new_two)


def solution(mesh):
    torus = Mesh(
        mesh.devices.reshape(SIDE, SIDE, 2, mesh.shape["fsdp"]), (*DP, "fsdp")
    )
    placed = (P(DP, "fsdp"), P(DP, None), P(DP, "fsdp"), P(DP, "fsdp"), P(DP, "fsdp"))
    return jax.shard_map(
        shards,
        mesh=torus,
        in_specs=placed,
        out_specs=(P(None, "fsdp"), P(DP, "fsdp"), P(DP, "fsdp"), P(DP, "fsdp")),
        check_vma=False,
    )
```

```python
import functools

import jax
import jax.numpy as jnp
from jax import lax
from jax.experimental import pallas as pl
from jax.experimental.pallas import tpu as pltpu
from jax.sharding import Mesh
from jax.sharding import PartitionSpec as P

CHIPS = ("dp_0", "dp_1")
CORE = "dp_2"
DP = (*CHIPS, CORE)
SIDE = 4
SWAP = [(0, 1), (1, 0)]
VMEM = pl.BlockSpec(memory_space=pltpu.VMEM)
HBM = pl.BlockSpec(memory_space=pl.ANY)
BF16, F32 = jnp.bfloat16, jnp.float32


def near(value):
    return pltpu.with_memory_space_constraint(value, pltpu.VMEM)


def far(value):
    return pltpu.with_memory_space_constraint(value, pltpu.HBM)


def call(body, outs, args, flops=0, moved=0, specs=None, out_specs=None, **more):
    return pl.pallas_call(
        body,
        out_shape=outs,
        in_specs=specs or [VMEM] * len(args),
        out_specs=out_specs or [VMEM] * len(outs),
        cost_estimate=pl.CostEstimate(flops=flops, bytes_accessed=moved, transcendentals=0),
        compiler_params=pltpu.CompilerParams(vmem_limit_bytes=24 * 2**20),
        **more,
    )(*args)


def product(left, right):
    return lax.dot_general(left, right, (((0,), (0,)), ((), ())), preferred_element_type=F32)


def core_columns(half):
    here = lax.axis_index(CORE)
    own = pl.ds(pl.multiple_of(here * half, half), half)
    return own, pl.ds(pl.multiple_of((1 - here) * half, half), half)


def pieces(core, distant):
    row, column = (lax.axis_index(axis) for axis in CHIPS)
    pair = lax.bitwise_xor(lax.shift_right_logical(jnp.where(core == 0, column, row), 1), distant)
    starts = [
        jnp.where(core == 0, 256 * part + 128 * pair, 512 * pair + 128 * part)
        for part in range(SIDE)
    ]
    return [pl.ds(pl.multiple_of(start, 128), 128) for start in starts]


def load_and_multiply(chunks, lg_hbm, hid_hbm, lg, mine, distant, close, theirs, total, sems):
    tokens = lg.shape[0]
    step = tokens // chunks
    own, other = core_columns(mine.shape[1])
    copies = []
    for k in range(chunks):
        part = pl.ds(k * step, step)
        copies.append(
            (
                pltpu.make_async_copy(lg_hbm.at[part], lg.at[part], sems.at[k, 0]),
                pltpu.make_async_copy(hid_hbm.at[part, other], theirs.at[part], sems.at[k, 1]),
            )
        )
        for copy in copies[-1]:
            copy.start()
    last = pltpu.make_async_copy(hid_hbm.at[:, own], mine, sems.at[chunks, 0])
    last.start()
    core = 1 - lax.axis_index(CORE)
    for k in range(chunks):
        part = pl.ds(k * step, step)
        for copy in copies[k]:
            copy.wait()
        for number, out in ((1, distant), (0, close)):
            for place, block in enumerate(pieces(core, number)):
                here, there = pl.ds(512 * number + 128 * place, 128), pl.ds(128 * place, 128)
                value = product(lg[part, block], theirs[part, :])
                if k > 0:
                    value += total[here, :]
                if k < chunks - 1:
                    total[here, :] = value
                else:
                    out[there, :] = value.astype(BF16)
    last.wait()


def multiply(distant, lg, hid, out):
    for place, block in enumerate(pieces(lax.axis_index(CORE), distant)):
        out[pl.ds(128 * place, 128), :] = product(lg[:, block], hid[...]).astype(BF16)


def arrange(distant, kept, arrived, *outs):
    here, row, column = (lax.axis_index(axis) for axis in (CORE, *CHIPS))
    size = outs[0].shape[1]
    for mask, out in enumerate(outs):
        low = lax.bitwise_xor(jnp.where(here == 0, column, row), mask) & 1
        for place in range(SIDE):
            block = jnp.where(here == 0, 2 * place + low, SIDE * low + place)
            rows = pl.ds(pl.multiple_of(block * size, size), size)
            out[place] = (kept[rows, :].astype(F32) + arrived[rows, :].astype(F32)).astype(BF16)


def add_first(own, one, two, three, *outs):
    here, row, column = (lax.axis_index(axis) for axis in (CORE, *CHIPS))
    second = jnp.where(here == 0, row, column)
    for mask, out in enumerate(outs):
        place = lax.bitwise_xor(second, mask)
        total = own[place].astype(F32) + one[place].astype(F32)
        total += two[place].astype(F32) + three[place].astype(F32)
        out[...] = total.astype(out.dtype)


def add_second(own, one, two, three, grad, squares):
    value = own[...] + one[...].astype(F32) + two[...].astype(F32) + three[...].astype(F32)
    grad[...] = value
    square = value * value
    lanes = sum(square[:, first : first + 128] for first in range(0, value.shape[1], 128))
    squares[...] = jnp.broadcast_to(jnp.sum(lanes, axis=0, keepdims=True)[None], squares.shape)


def pack(*refs):
    (*sources, out) = refs
    _, other = core_columns(out.shape[2])
    for number, source in enumerate(sources):
        out[number] = source[:, other]


def update(entries, sums, grad, master, moment_one, moment_two, packed, values, kept, sent):
    here = lax.axis_index(CORE)
    rows, half = kept.shape[1:]
    own, _ = core_columns(half)
    sumsq = jnp.sum(jnp.sum(sums[...], axis=0, keepdims=True), axis=1, keepdims=True)
    factor = jnp.minimum(1.0, 1.0 / jnp.sqrt(sumsq / entries))
    owned = (master[:, own], moment_one[:, own], moment_two[:, own])
    lent = (packed[0], packed[1], packed[2])
    for core, (old, old_one, old_two), out in ((here, owned, kept), (1 - here, lent, sent)):
        place = pl.ds(pl.multiple_of(core * rows, rows), rows)
        clipped = factor * grad[place, :]
        one = 0.9 * old_one + 0.1 * clipped
        two = 0.95 * old_two + 0.05 * clipped * clipped
        first = one / (1.0 - 0.9**10)
        second = two / (1.0 - 0.95**10)
        value = old - 0.05 * (first / (jnp.sqrt(second) + 1e-08) + 0.1 * old)
        out[0], out[1], out[2] = value, one, two
        values[place, :] = value.astype(BF16)


def join(*refs):
    (*sources, out) = refs
    for number, source in enumerate(sources):
        out[number] = source[...]


def row_copies(source, second_mask, core, out, sems, number):
    row, column = (lax.axis_index(axis) for axis in CHIPS)
    size, half = source.shape[1:]
    columns = pl.ds(pl.multiple_of(core * half, half), half)
    copies = []
    for mask in range(SIDE):
        chip = jnp.where(
            core == 0,
            lax.bitwise_xor(row, mask) * SIDE + lax.bitwise_xor(column, second_mask),
            lax.bitwise_xor(row, second_mask) * SIDE + lax.bitwise_xor(column, mask),
        )
        rows = pl.ds(pl.multiple_of(chip * size, size), size)
        copies.append(
            pltpu.make_async_copy(source.at[mask], out.at[rows, columns], sems.at[number + mask])
        )
    return copies


def write_first(own, arrived, kept, given, out, new_master, new_one, new_two, sems):
    here = lax.axis_index(CORE)
    copies = row_copies(own, 0, here, out, sems, 0)
    copies += row_copies(arrived, 0, 1 - here, out, sems, len(copies))
    for source, columns in zip((kept, given), core_columns(kept.shape[2])):
        for number, target in enumerate((new_master, new_one, new_two)):
            copies.append(
                pltpu.make_async_copy(
                    source.at[number], target.at[:, columns], sems.at[len(copies)]
                )
            )
    for copy in copies:
        copy.start()
    for copy in copies:
        copy.wait()


def write_rest(other, *refs):
    (*sources, _, out, sems) = refs
    here = lax.axis_index(CORE)
    core = 1 - here if other else here
    copies = []
    for mask, source in enumerate(sources, 1):
        copies += row_copies(source, mask, core, out, sems, len(copies))
    for copy in copies:
        copy.start()
    for copy in copies:
        copy.wait()


def partners(mask, stage):
    pairs = []
    for row in range(SIDE):
        for column in range(SIDE):
            for core in range(2):
                place = (row * SIDE + column) * 2 + core
                if core == stage:
                    other = (row * SIDE + (column ^ mask)) * 2 + core
                else:
                    other = ((row ^ mask) * SIDE + column) * 2 + core
                pairs.append((place, other))
    return pairs


def shards(hidden, logit_grad, master, moment_one, moment_two):
    rows, columns = master.shape
    tokens, total_rows = logit_grad.shape
    half = columns // 2
    everyone = (*DP, "fsdp")
    count = lax.axis_size(everyone)
    width = columns * lax.axis_size("fsdp")
    work = 2 * tokens * total_rows * half

    chunks = 4
    lg, mine, *sent = call(
        functools.partial(load_and_multiply, chunks),
        [
            pltpu.VMEM((tokens, total_rows), BF16),
            pltpu.VMEM((tokens, half), BF16),
            pltpu.VMEM((total_rows // 2, half), BF16),
            pltpu.VMEM((total_rows // 2, half), BF16),
        ],
        [far(logit_grad), far(hidden)],
        flops=work,
        moved=4 * tokens * columns,
        specs=[HBM, HBM],
        scratch_shapes=[
            pltpu.VMEM((tokens, half), BF16),
            pltpu.VMEM((total_rows, half), F32),
            pltpu.SemaphoreType.DMA((chunks + 1, 2)),
        ],
    )
    blocks = []
    for distant, value in zip((1, 0), sent):
        arrived = lax.ppermute(value, CORE, SWAP)
        (kept,) = call(
            functools.partial(multiply, distant),
            [pltpu.VMEM((total_rows // 2, half), BF16)],
            [near(lg), near(mine)],
            flops=work // 2,
            moved=tokens * columns,
        )
        blocks = [
            *call(
                functools.partial(arrange, distant),
                [pltpu.VMEM((SIDE, 2 * rows, half), BF16)] * 2,
                [near(kept), near(arrived)],
            ),
            *blocks,
        ]
    first = [blocks[0]] + [
        lax.ppermute(blocks[mask], DP, partners(mask, 0)) for mask in (2, 3, 1)
    ]
    *states, _ = lax.optimization_barrier((master, moment_one, moment_two, first[1]))
    (lent,) = call(
        pack, [pltpu.VMEM((3, rows, half), F32)], [near(state) for state in states]
    )
    packed = lax.ppermute(lent, CORE, SWAP)
    totals = call(
        add_first,
        [pltpu.VMEM((2 * rows, half), F32)] + [pltpu.VMEM((2 * rows, half), BF16)] * (SIDE - 1),
        [near(value) for value in first],
    )
    second = [totals[0]] + [
        lax.ppermute(totals[mask], DP, partners(mask, 1)) for mask in (2, 1, 3)
    ]
    grad, copies = call(
        add_second,
        [pltpu.VMEM((2 * rows, half), F32), pltpu.VMEM((count, 1, 128), F32)],
        [near(value) for value in second],
    )
    copies, packed = lax.optimization_barrier((copies, packed))
    sums = lax.all_to_all(copies, everyone, 0, 0, tiled=True).reshape(count, 128)

    values, kept, sent = call(
        functools.partial(update, float(total_rows * width)),
        [pltpu.VMEM((2 * rows, half), BF16)] + [pltpu.VMEM((3, rows, half), F32)] * 2,
        [near(value) for value in (sums, grad, *states, packed)],
    )
    line = {mask: lax.ppermute(values, DP, partners(mask, 1)) for mask in (1, 3, 2)}
    line = [values] + [line[mask] for mask in range(1, SIDE)]
    (joined,) = call(
        join, [pltpu.VMEM((SIDE, 2 * rows, half), BF16)], [near(value) for value in line]
    )
    given = lax.ppermute(sent, CORE, SWAP)
    plane = {mask: lax.ppermute(joined, DP, partners(mask, 0)) for mask in (1, 3, 2)}
    plane = [joined] + [plane[mask] for mask in range(1, SIDE)]
    plane[2], given = lax.optimization_barrier((plane[2], given))
    across = lax.ppermute(joined, CORE, SWAP)
    slab = pltpu.HBM((total_rows, columns), BF16)
    new_rows, new_master, new_one, new_two = call(
        write_first,
        [slab] + [pltpu.HBM((rows, columns), F32)] * 3,
        [near(value) for value in (joined, across, kept, given)],
        moved=total_rows * columns,
        out_specs=[HBM] * 4,
        scratch_shapes=[pltpu.SemaphoreType.DMA((2 * SIDE + 6,))],
    )
    plane[1], new_rows = lax.optimization_barrier((plane[1], new_rows))
    others = [lax.ppermute(value, CORE, SWAP) for value in plane[1:]]
    for other, sources in enumerate((plane[1:], others)):
        (new_rows,) = call(
            functools.partial(write_rest, other),
            [slab],
            [*(near(value) for value in sources), far(new_rows)],
            moved=total_rows * columns,
            specs=[VMEM] * (SIDE - 1) + [HBM],
            out_specs=[HBM],
            scratch_shapes=[pltpu.SemaphoreType.DMA((SIDE * (SIDE - 1),))],
            input_output_aliases={SIDE - 1: 0},
        )
    return (new_rows, new_master, new_one, new_two)


def solution(mesh):
    torus = Mesh(
        mesh.devices.reshape(SIDE, SIDE, 2, mesh.shape["fsdp"]), (*DP, "fsdp")
    )
    placed = (P(DP, "fsdp"), P(DP, None), P(DP, "fsdp"), P(DP, "fsdp"), P(DP, "fsdp"))
    return jax.shard_map(
        shards,
        mesh=torus,
        in_specs=placed,
        out_specs=(P(None, "fsdp"), P(DP, "fsdp"), P(DP, "fsdp"), P(DP, "fsdp")),
        check_vma=False,
    )
```

```python
import functools

import jax
import jax.numpy as jnp
from jax import lax
from jax.experimental import pallas as pl
from jax.experimental.pallas import tpu as pltpu
from jax.sharding import Mesh
from jax.sharding import PartitionSpec as P

CHIPS = ("dp_0", "dp_1")
CORE = "dp_2"
DP = (*CHIPS, CORE)
SIDE = 4
SWAP = [(0, 1), (1, 0)]
VMEM = pl.BlockSpec(memory_space=pltpu.VMEM)
HBM = pl.BlockSpec(memory_space=pl.ANY)
BF16, F32 = jnp.bfloat16, jnp.float32


def near(value):
    return pltpu.with_memory_space_constraint(value, pltpu.VMEM)


def far(value):
    return pltpu.with_memory_space_constraint(value, pltpu.HBM)


def call(body, outs, args, flops=0, moved=0, specs=None, out_specs=None, **more):
    return pl.pallas_call(
        body,
        out_shape=outs,
        in_specs=specs or [VMEM] * len(args),
        out_specs=out_specs or [VMEM] * len(outs),
        cost_estimate=pl.CostEstimate(flops=flops, bytes_accessed=moved, transcendentals=0),
        compiler_params=pltpu.CompilerParams(vmem_limit_bytes=24 * 2**20),
        **more,
    )(*args)


def product(left, right):
    return lax.dot_general(left, right, (((0,), (0,)), ((), ())), preferred_element_type=F32)


def core_columns(half):
    here = lax.axis_index(CORE)
    own = pl.ds(pl.multiple_of(here * half, half), half)
    return own, pl.ds(pl.multiple_of((1 - here) * half, half), half)


def pieces(core, distant):
    row, column = (lax.axis_index(axis) for axis in CHIPS)
    pair = lax.bitwise_xor(lax.shift_right_logical(jnp.where(core == 0, column, row), 1), distant)
    starts = [
        jnp.where(core == 0, 256 * part + 128 * pair, 512 * pair + 128 * part)
        for part in range(SIDE)
    ]
    return [pl.ds(pl.multiple_of(start, 128), 128) for start in starts]


def load_and_multiply(chunks, lg_hbm, hid_hbm, lg, mine, distant, close, theirs, total, sems):
    tokens = lg.shape[0]
    step = tokens // chunks
    own, other = core_columns(mine.shape[1])
    copies = []
    for k in range(chunks):
        part = pl.ds(k * step, step)
        copies.append(
            (
                pltpu.make_async_copy(lg_hbm.at[part], lg.at[part], sems.at[k, 0]),
                pltpu.make_async_copy(hid_hbm.at[part, other], theirs.at[part], sems.at[k, 1]),
            )
        )
        for copy in copies[-1]:
            copy.start()
    last = pltpu.make_async_copy(hid_hbm.at[:, own], mine, sems.at[chunks, 0])
    last.start()
    core = 1 - lax.axis_index(CORE)
    for k in range(chunks):
        part = pl.ds(k * step, step)
        for copy in copies[k]:
            copy.wait()
        for number, out in ((1, distant), (0, close)):
            for place, block in enumerate(pieces(core, number)):
                here, there = pl.ds(512 * number + 128 * place, 128), pl.ds(128 * place, 128)
                value = product(lg[part, block], theirs[part, :])
                if k > 0:
                    value += total[here, :]
                if k < chunks - 1:
                    total[here, :] = value
                else:
                    out[there, :] = value.astype(BF16)
    last.wait()


def multiply(distant, lg, hid, out):
    for place, block in enumerate(pieces(lax.axis_index(CORE), distant)):
        out[pl.ds(128 * place, 128), :] = product(lg[:, block], hid[...]).astype(BF16)


def arrange(distant, kept, arrived, *outs):
    here, row, column = (lax.axis_index(axis) for axis in (CORE, *CHIPS))
    size = outs[0].shape[1]
    for mask, out in enumerate(outs):
        low = lax.bitwise_xor(jnp.where(here == 0, column, row), mask) & 1
        for place in range(SIDE):
            block = jnp.where(here == 0, 2 * place + low, SIDE * low + place)
            rows = pl.ds(pl.multiple_of(block * size, size), size)
            out[place] = (kept[rows, :].astype(F32) + arrived[rows, :].astype(F32)).astype(BF16)


def add_first(own, one, two, three, *outs):
    here, row, column = (lax.axis_index(axis) for axis in (CORE, *CHIPS))
    second = jnp.where(here == 0, row, column)
    for mask, out in enumerate(outs):
        place = lax.bitwise_xor(second, mask)
        total = own[place].astype(F32) + one[place].astype(F32)
        total += two[place].astype(F32) + three[place].astype(F32)
        out[...] = total.astype(out.dtype)


def add_second(own, one, two, three, grad, squares):
    value = own[...] + one[...].astype(F32) + two[...].astype(F32) + three[...].astype(F32)
    grad[...] = value
    square = value * value
    lanes = sum(square[:, first : first + 128] for first in range(0, value.shape[1], 128))
    squares[...] = jnp.broadcast_to(jnp.sum(lanes, axis=0, keepdims=True)[None], squares.shape)


def pack(*refs):
    (*sources, out) = refs
    _, other = core_columns(out.shape[2])
    for number, source in enumerate(sources):
        out[number] = source[:, other]


def update(entries, sums, grad, master, moment_one, moment_two, packed, values, kept, sent):
    here = lax.axis_index(CORE)
    rows, half = kept.shape[1:]
    own, _ = core_columns(half)
    sumsq = jnp.sum(jnp.sum(sums[...], axis=0, keepdims=True), axis=1, keepdims=True)
    factor = jnp.minimum(1.0, 1.0 / jnp.sqrt(sumsq / entries))
    owned = (master[:, own], moment_one[:, own], moment_two[:, own])
    lent = (packed[0], packed[1], packed[2])
    for core, (old, old_one, old_two), out in ((here, owned, kept), (1 - here, lent, sent)):
        place = pl.ds(pl.multiple_of(core * rows, rows), rows)
        clipped = factor * grad[place, :]
        one = 0.9 * old_one + 0.1 * clipped
        two = 0.95 * old_two + 0.05 * clipped * clipped
        first = one / (1.0 - 0.9**10)
        second = two / (1.0 - 0.95**10)
        value = old - 0.05 * (first / (jnp.sqrt(second) + 1e-08) + 0.1 * old)
        out[0], out[1], out[2] = value, one, two
        values[place, :] = value.astype(BF16)


def join(*refs):
    (*sources, out) = refs
    for number, source in enumerate(sources):
        out[number] = source[...]


def row_copies(source, second_mask, core, out, sems, number):
    row, column = (lax.axis_index(axis) for axis in CHIPS)
    size, half = source.shape[1:]
    columns = pl.ds(pl.multiple_of(core * half, half), half)
    copies = []
    for mask in range(SIDE):
        chip = jnp.where(
            core == 0,
            lax.bitwise_xor(row, mask) * SIDE + lax.bitwise_xor(column, second_mask),
            lax.bitwise_xor(row, second_mask) * SIDE + lax.bitwise_xor(column, mask),
        )
        rows = pl.ds(pl.multiple_of(chip * size, size), size)
        copies.append(
            pltpu.make_async_copy(source.at[mask], out.at[rows, columns], sems.at[number + mask])
        )
    return copies


def write_first(own, arrived, kept, given, out, new_master, new_one, new_two, sems):
    here = lax.axis_index(CORE)
    copies = row_copies(own, 0, here, out, sems, 0)
    copies += row_copies(arrived, 0, 1 - here, out, sems, len(copies))
    for source, columns in zip((kept, given), core_columns(kept.shape[2])):
        for number, target in enumerate((new_master, new_one, new_two)):
            copies.append(
                pltpu.make_async_copy(
                    source.at[number], target.at[:, columns], sems.at[len(copies)]
                )
            )
    for copy in copies:
        copy.start()
    for copy in copies:
        copy.wait()


def write_rest(other, *refs):
    (*sources, _, out, sems) = refs
    here = lax.axis_index(CORE)
    core = 1 - here if other else here
    copies = []
    for mask, source in enumerate(sources, 1):
        copies += row_copies(source, mask, core, out, sems, len(copies))
    for copy in copies:
        copy.start()
    for copy in copies:
        copy.wait()


def partners(mask, stage):
    pairs = []
    for row in range(SIDE):
        for column in range(SIDE):
            for core in range(2):
                place = (row * SIDE + column) * 2 + core
                if core == stage:
                    other = (row * SIDE + (column ^ mask)) * 2 + core
                else:
                    other = ((row ^ mask) * SIDE + column) * 2 + core
                pairs.append((place, other))
    return pairs


def shards(hidden, logit_grad, master, moment_one, moment_two):
    rows, columns = master.shape
    tokens, total_rows = logit_grad.shape
    half = columns // 2
    everyone = (*DP, "fsdp")
    count = lax.axis_size(everyone)
    width = columns * lax.axis_size("fsdp")
    work = 2 * tokens * total_rows * half

    chunks = 4
    lg, mine, *sent = call(
        functools.partial(load_and_multiply, chunks),
        [
            pltpu.VMEM((tokens, total_rows), BF16),
            pltpu.VMEM((tokens, half), BF16),
            pltpu.VMEM((total_rows // 2, half), BF16),
            pltpu.VMEM((total_rows // 2, half), BF16),
        ],
        [far(logit_grad), far(hidden)],
        flops=work,
        moved=4 * tokens * columns,
        specs=[HBM, HBM],
        scratch_shapes=[
            pltpu.VMEM((tokens, half), BF16),
            pltpu.VMEM((total_rows, half), F32),
            pltpu.SemaphoreType.DMA((chunks + 1, 2)),
        ],
    )
    blocks = []
    for distant, value in zip((1, 0), sent):
        arrived = lax.ppermute(value, CORE, SWAP)
        (kept,) = call(
            functools.partial(multiply, distant),
            [pltpu.VMEM((total_rows // 2, half), BF16)],
            [near(lg), near(mine)],
            flops=work // 2,
            moved=tokens * columns,
        )
        blocks = [
            *call(
                functools.partial(arrange, distant),
                [pltpu.VMEM((SIDE, 2 * rows, half), BF16)] * 2,
                [near(kept), near(arrived)],
            ),
            *blocks,
        ]
    first = [blocks[0]] + [
        lax.ppermute(blocks[mask], DP, partners(mask, 0)) for mask in (2, 1, 3)
    ]
    *states, _ = lax.optimization_barrier((master, moment_one, moment_two, first[1]))
    (lent,) = call(
        pack, [pltpu.VMEM((3, rows, half), F32)], [near(state) for state in states]
    )
    packed = lax.ppermute(lent, CORE, SWAP)
    totals = call(
        add_first,
        [pltpu.VMEM((2 * rows, half), F32)] + [pltpu.VMEM((2 * rows, half), BF16)] * (SIDE - 1),
        [near(value) for value in first],
    )
    second = [totals[0]] + [
        lax.ppermute(totals[mask], DP, partners(mask, 1)) for mask in (2, 1, 3)
    ]
    grad, copies = call(
        add_second,
        [pltpu.VMEM((2 * rows, half), F32), pltpu.VMEM((count, 1, 128), F32)],
        [near(value) for value in second],
    )
    copies, packed = lax.optimization_barrier((copies, packed))
    sums = lax.all_to_all(copies, everyone, 0, 0, tiled=True).reshape(count, 128)

    values, kept, sent = call(
        functools.partial(update, float(total_rows * width)),
        [pltpu.VMEM((2 * rows, half), BF16)] + [pltpu.VMEM((3, rows, half), F32)] * 2,
        [near(value) for value in (sums, grad, *states, packed)],
    )
    line = {mask: lax.ppermute(values, DP, partners(mask, 1)) for mask in (1, 3, 2)}
    line = [values] + [line[mask] for mask in range(1, SIDE)]
    (joined,) = call(
        join, [pltpu.VMEM((SIDE, 2 * rows, half), BF16)], [near(value) for value in line]
    )
    given = lax.ppermute(sent, CORE, SWAP)
    plane = {mask: lax.ppermute(joined, DP, partners(mask, 0)) for mask in (1, 3, 2)}
    plane = [joined] + [plane[mask] for mask in range(1, SIDE)]
    plane[2], given = lax.optimization_barrier((plane[2], given))
    across = lax.ppermute(joined, CORE, SWAP)
    slab = pltpu.HBM((total_rows, columns), BF16)
    new_rows, new_master, new_one, new_two = call(
        write_first,
        [slab] + [pltpu.HBM((rows, columns), F32)] * 3,
        [near(value) for value in (joined, across, kept, given)],
        moved=total_rows * columns,
        out_specs=[HBM] * 4,
        scratch_shapes=[pltpu.SemaphoreType.DMA((2 * SIDE + 6,))],
    )
    plane[1], new_rows = lax.optimization_barrier((plane[1], new_rows))
    others = [lax.ppermute(value, CORE, SWAP) for value in plane[1:]]
    for other, sources in enumerate((plane[1:], others)):
        (new_rows,) = call(
            functools.partial(write_rest, other),
            [slab],
            [*(near(value) for value in sources), far(new_rows)],
            moved=total_rows * columns,
            specs=[VMEM] * (SIDE - 1) + [HBM],
            out_specs=[HBM],
            scratch_shapes=[pltpu.SemaphoreType.DMA((SIDE * (SIDE - 1),))],
            input_output_aliases={SIDE - 1: 0},
        )
    return (new_rows, new_master, new_one, new_two)


def solution(mesh):
    torus = Mesh(
        mesh.devices.reshape(SIDE, SIDE, 2, mesh.shape["fsdp"]), (*DP, "fsdp")
    )
    placed = (P(DP, "fsdp"), P(DP, None), P(DP, "fsdp"), P(DP, "fsdp"), P(DP, "fsdp"))
    return jax.shard_map(
        shards,
        mesh=torus,
        in_specs=placed,
        out_specs=(P(None, "fsdp"), P(DP, "fsdp"), P(DP, "fsdp"), P(DP, "fsdp")),
        check_vma=False,
    )
```
